32 devices in a mesh: dp: 8 (over y, x, core), ctx: 4 (over z).
Axes of the slice: x: 2, y: 2, z: 4, core: 2. Of those that a mesh axis runs over, the one named last changes fastest.
Arguments:
- hidden: bfloat16 [8, 1536, 8192], P('dp', 'ctx'), may hold values from -6 to 6
- queries: bfloat16 [8, 1536, 4096], P('dp', 'ctx'), may hold values from -136 to 136
- weights_old: float32 [8192, 1024], P(('dp', 'ctx')), may hold values from -0.0625 to 0.0625
- gradient_old: float32 [8192, 1024], P(('dp', 'ctx')), may hold values from -6 to 6
- first_old: float32 [8192, 1024], P(('dp', 'ctx')), may hold values from -4 to 4
- second_old: float32 [8192, 1024], P(('dp', 'ctx')), may hold values from 0.25 to 4
- old_owner: int32 [32], replicated, may hold values from 0 to 31, each once
- new_owner: int32 [32], replicated, may hold values from 0 to 31, each once
- offsets: int32 [8, 4, 2], P('dp'), may hold values from 0 to 1344, as said below
Outputs:
- weights_new: float32 [1024, 8192], P(('dp', 'ctx'))
- first_new: float32 [1024, 8192], P(('dp', 'ctx'))
- second_new: float32 [1024, 8192], P(('dp', 'ctx'))
- attended: bfloat16 [8, 1536, 4096], P('dp', 'ctx')
The draws below stay inside these ranges and needn't reach their ends.
Inputs may be any that keep to these rules, and one draw needn't show every extreme that they name: `offsets`: for sequence b and ctx index c the two entries are p * 192 and (7 - p) * 192, where p runs over a permutation of the ctx indices drawn for each sequence. `old_owner`: each block index appears once. `new_owner`: each block index appears once.
All inputs are finite; a program needn't handle non-finite values.
Results may differ from the reference program's by a relative error of at most 0.0055.
The reference program's roundings to bfloat16 on the way count: a program that leaves them out, or rounds other values in their place, can miss the bound.
Values may be sent and summed in bfloat16 or wider, within the bound.
A program may use at most 320 MiB of HBM per device.

```python
import math
import jax
import jax.numpy as jnp
from jax import lax

D = 8192
HEAD = 128
KV_HEADS = 4
Q_HEADS = 32
TOK = 384
HALF = 192
SEQ = 1536
BATCH = 8
PROJ = 1024
ROW_BLOCK = 256
COL_BLOCK = 32


def draw_queries(key, part):
    shape = (BATCH, SEQ, Q_HEADS * HEAD)
    normal_part = jax.random.normal(key, shape, jnp.float32)
    return jnp.clip(normal_part, -6.0, 6.0).astype(jnp.bfloat16)


def draw_offsets(key, part):
    ctx_count = SEQ // TOK
    half_tok = TOK // 2
    subkeys = jax.random.split(key, BATCH)

    def order_of(subkey):
        return jax.random.permutation(subkey, ctx_count)
    orders = jax.vmap(order_of)(subkeys).astype(jnp.int32)
    first_start = orders * half_tok
    second_start = (2 * ctx_count - 1 - orders) * half_tok
    return jnp.stack([first_start, second_start], axis=-1).astype(jnp.int32)


def levels(key, dims, cuts, smallest, high):
    factor_of, own = 1.0, jax.random.fold_in(key, 6)
    for dim, shards_of in cuts:
        heights = jnp.exp(jax.random.uniform(jax.random.fold_in(own, dim), (shards_of,), jnp.float32, smallest / len(cuts), high / len(cuts)))
        factor_of = factor_of * jnp.repeat(heights, dims[dim] // shards_of).reshape([-1 if axis == dim else 1 for axis in range(len(dims))])
    return factor_of


def gaussian(key, dims, width, limit, cuts=(), kind=jnp.bfloat16):
    result = width * jax.random.normal(key, dims, jnp.float32)
    if cuts:
        result = result * levels(key, dims, cuts, -0.22, 0.18)
    return jnp.clip(result, -limit, limit).astype(kind)


def setup_inputs(seed: int = 0) -> dict:
    splits = jax.random.split(jax.random.key(seed), 10)
    hidden = gaussian(splits[0], (BATCH, SEQ, D), 1.0, 6.0, ((0, 8), (1, 4)))
    queries = draw_queries(jax.random.fold_in(splits[9], 71), 0)
    weights_old = gaussian(splits[2], (D, PROJ), D ** -0.5, 0.0625, ((0, 32),), jnp.float32)
    gradient_old = gaussian(splits[3], (D, PROJ), 1.0, 6.0, ((0, 32),), jnp.float32)
    first_old = gaussian(splits[4], (D, PROJ), 0.3, 4.0, ((0, 32),), jnp.float32)
    second_old = jnp.clip(jnp.exp(math.log(4.0) - 2.7725887 * jax.random.uniform(splits[5], (D, PROJ), jnp.float32) ** levels(splits[5], (D, PROJ), ((0, 32),), -0.2, 0.2)), 0.25, 4.0)
    old_owner = jax.random.permutation(splits[6], D // ROW_BLOCK).astype(jnp.int32)
    new_owner = jax.random.permutation(splits[7], D // ROW_BLOCK).astype(jnp.int32)
    offsets = draw_offsets(jax.random.fold_in(splits[9], 71), 0)
    return dict(hidden=hidden, queries=queries, weights_old=weights_old, gradient_old=gradient_old, first_old=first_old, second_old=second_old, old_owner=old_owner, new_owner=new_owner, offsets=offsets)


learn_rate = 0.0003
beta_one = 0.9
beta_two = 0.95
adam_eps = 1e-08
decay_rate = 0.1
step_number = 1000
corr_one = 1.0 - beta_one ** step_number
corr_two = 1.0 - beta_two ** step_number
rope_base = 500000.0

def adam_step(weights, gradient, first_mom, second_mom):
    first_next = beta_one * first_mom + (1.0 - beta_one) * gradient
    second_next = beta_two * second_mom + (1.0 - beta_two) * gradient * gradient
    direction = first_next / corr_one / (jnp.sqrt(second_next / corr_two) + adam_eps)
    weights_next = weights - learn_rate * (direction + decay_rate * weights)
    return (weights_next, first_next, second_next)

def rotate_keys(key_heads, positions):
    head_dim = key_heads.shape[-1]
    half_dim = head_dim // 2
    exponent = jnp.arange(half_dim, dtype=jnp.float32) * (2.0 / head_dim)
    inv_freq = jnp.power(rope_base, -exponent)
    angles = positions.astype(jnp.float32)[..., None] * inv_freq
    cosine = jnp.cos(angles)[..., None, :]
    sine_part = jnp.sin(angles)[..., None, :]
    first_half = key_heads[..., :half_dim]
    second_half = key_heads[..., half_dim:]
    return jnp.concatenate([first_half * cosine - second_half * sine_part, second_half * cosine + first_half * sine_part], axis=-1)

def reference(hidden, queries, weights_old, gradient_old, first_old, second_old, old_owner, new_owner, offsets):
    devices = D // ROW_BLOCK

    def to_logical(stored):
        blocks = stored.reshape(devices, ROW_BLOCK, PROJ)
        return jnp.zeros_like(blocks).at[old_owner].set(blocks).reshape(D, PROJ)

    def to_new(logical):
        return jnp.take(logical.T.reshape(devices, COL_BLOCK, D), new_owner, axis=0).reshape(PROJ, D)
    weights_next, first_next, second_next = adam_step(to_logical(weights_old), to_logical(gradient_old), to_logical(first_old), to_logical(second_old))
    copies = weights_next.astype(jnp.bfloat16)
    row_ids = jnp.arange(SEQ, dtype=jnp.int32)
    local_row = row_ids % TOK
    positions = offsets[:, row_ids // TOK, local_row // HALF] + local_row % HALF
    key_width = KV_HEADS * HEAD
    groups = Q_HEADS // KV_HEADS

    def one_sequence(packed):
        tokens, query_rows, token_pos = packed
        projected = jnp.dot(tokens, copies, preferred_element_type=jnp.float32)
        key_heads = rotate_keys(projected[:, :key_width].reshape(SEQ, KV_HEADS, HEAD), token_pos)
        key_round = lax.optimization_barrier(key_heads.astype(jnp.bfloat16)).astype(jnp.float32)
        value_round = lax.optimization_barrier(projected[:, key_width:].astype(jnp.bfloat16)).astype(jnp.float32).reshape(SEQ, KV_HEADS, HEAD)
        query_heads = query_rows.astype(jnp.float32).reshape(SEQ, KV_HEADS, groups, HEAD)
        visible = token_pos[None, :] <= token_pos[:, None]

        def one_head(inputs):
            query_group, key_head, value_head = inputs
            scores = jnp.einsum('tgd,nd->gtn', query_group, key_head) / math.sqrt(HEAD)
            masked = jnp.where(visible[None], scores, -jnp.inf)
            best_score = lax.optimization_barrier(jnp.max(masked, axis=2, keepdims=True))
            weights = jnp.where(visible[None], jnp.exp(masked - best_score), 0.0)
            rounded = lax.optimization_barrier(weights.astype(jnp.bfloat16)).astype(jnp.float32)
            numerator = jnp.einsum('gtn,nd->tgd', rounded, value_head)
            return numerator / lax.optimization_barrier(jnp.sum(weights, axis=2)).T[:, :, None]
        heads_out = lax.map(one_head, (query_heads.transpose(1, 0, 2, 3), key_round.transpose(1, 0, 2), value_round.transpose(1, 0, 2)))
        return heads_out.transpose(1, 0, 2, 3).reshape(SEQ, Q_HEADS * HEAD).astype(jnp.bfloat16)
    attended = lax.map(one_sequence, (hidden, queries, positions))
    return (to_new(weights_next), to_new(first_next), to_new(second_next), attended)
```

```python
import functools
import math

import jax
import jax.numpy as jnp
from jax import lax
from jax.experimental import pallas as pl
from jax.experimental.pallas import tpu as pltpu
from jax.sharding import PartitionSpec as P

HEAD = 128
KV_HEADS = 4
Q_HEADS = 32
GROUPS = Q_HEADS // KV_HEADS
CHUNKS = 2
LANES = 128
VMEM_LIMIT = 48 * 1024 * 1024

learn_rate = 0.0003
beta_one = 0.9
beta_two = 0.95
adam_eps = 1e-08
decay_rate = 0.1
step_number = 1000
corr_one = 1.0 - beta_one**step_number
corr_two = 1.0 - beta_two**step_number
rope_base = 500000.0


def moments(gradient, first_mom, second_mom):
    first_next = beta_one * first_mom + (1.0 - beta_one) * gradient
    second_next = beta_two * second_mom + (1.0 - beta_two) * gradient * gradient
    return first_next, second_next


def update(weights, first_next, second_next):
    direction = first_next / corr_one / (jnp.sqrt(second_next / corr_two) + adam_eps)
    return weights - learn_rate * (direction + decay_rate * weights)


def invert(owners):
    ids = jnp.arange(owners.shape[0], dtype=jnp.int32)
    return jnp.sum(jnp.where(owners[None, :] == ids[:, None], ids[None, :], 0), axis=1)


def moments_kernel(new_owner, g_ref, m_ref, v_ref, out_ref, first_t, second_t):
    first_next, second_next = moments(g_ref[...], m_ref[...], v_ref[...])
    first_t[...] = first_next.T
    second_t[...] = second_next.T
    devices, both, _ = out_ref.shape
    cols = both // 2

    def body(dest, carry):
        rows = pl.ds(pl.multiple_of(new_owner[dest] * cols, cols), cols)
        out_ref[dest] = jnp.concatenate([first_t[rows], second_t[rows]], axis=0).astype(out_ref.dtype)
        return carry

    lax.fori_loop(0, devices, body, 0)


def outgoing_moments(new_owner, gradient, first_mom, second_mom):
    rows, width = gradient.shape
    devices = new_owner.shape[0]
    whole = pl.BlockSpec(memory_space=pltpu.VMEM)
    return pl.pallas_call(
        moments_kernel,
        out_shape=jax.ShapeDtypeStruct((devices, 2 * width // devices, rows), jnp.bfloat16),
        in_specs=[pl.BlockSpec(memory_space=pltpu.SMEM), whole, whole, whole],
        out_specs=whole,
        scratch_shapes=[pltpu.VMEM((width, rows), jnp.float32)] * 2,
        compiler_params=pltpu.CompilerParams(vmem_limit_bytes=VMEM_LIMIT),
        cost_estimate=pl.CostEstimate(flops=10 * rows * width, bytes_accessed=16 * rows * width, transcendentals=0),
        name="moments",
    )(new_owner, gradient, first_mom, second_mom)


def order_kernel(inverse, in_ref, first_ref, second_ref):
    devices, both, rows = in_ref.shape
    cols = both // 2
    for block in range(devices):
        value = in_ref[inverse[block]].astype(jnp.float32)
        first_ref[:, block * rows : (block + 1) * rows] = value[:cols]
        second_ref[:, block * rows : (block + 1) * rows] = value[cols:]


def ordered_moments(inverse, incoming):
    devices, both, rows = incoming.shape
    whole = pl.BlockSpec(memory_space=pltpu.VMEM)
    shape = jax.ShapeDtypeStruct((both // 2, devices * rows), jnp.float32)
    return pl.pallas_call(
        order_kernel,
        out_shape=(shape, shape),
        in_specs=[pl.BlockSpec(memory_space=pltpu.SMEM), whole],
        out_specs=(whole, whole),
        compiler_params=pltpu.CompilerParams(vmem_limit_bytes=VMEM_LIMIT),
        cost_estimate=pl.CostEstimate(flops=0, bytes_accessed=6 * devices * both * rows, transcendentals=0),
        name="order",
    )(inverse, incoming)


def project_kernel(parts, inverse, feature, hidden_ref, cos_ref, sin_ref, *refs):
    w_refs, new_ref, outs, total = refs[:parts], refs[parts], refs[parts + 1 : -1], refs[-1]
    step = pl.program_id(0)
    block = jnp.concatenate([w[...] for w in w_refs], axis=0)
    term = jnp.dot(hidden_ref[...], block, preferred_element_type=jnp.float32)

    @pl.when(step == 0)
    def _():
        total[...] = term

    @pl.when(step > 0)
    def _():
        total[...] += term

    cols = new_ref.shape[0]
    first = feature[0] * cols
    base = pl.multiple_of(first // LANES * LANES, LANES)
    lanes = jnp.concatenate([w[:, pl.ds(base, LANES)] for w in w_refs], axis=0)
    here = lax.broadcasted_iota(jnp.int32, (cols, LANES), 1)
    want = lax.broadcasted_iota(jnp.int32, (cols, LANES), 0) + (first - base)
    pick = (here == want).astype(jnp.float32).astype(jnp.bfloat16)
    new_ref[...] = lax.dot_general(pick, lanes, (((1,), (1,)), ((), ())), preferred_element_type=jnp.float32)

    @pl.when(step == pl.num_programs(0) - 1)
    def _():
        cosine, sine = cos_ref[...], sin_ref[...]
        per = KV_HEADS // len(outs)
        for head in range(KV_HEADS):
            key = total[:, head * HEAD : (head + 1) * HEAD]
            turned = jnp.concatenate([key[:, HEAD // 2 :], key[:, : HEAD // 2]], axis=1)
            value = total[:, (KV_HEADS + head) * HEAD : (KV_HEADS + head + 1) * HEAD]
            out, at = outs[head // per], head % per * 2 * HEAD
            out[:, at : at + HEAD] = (key * cosine + turned * sine).astype(jnp.bfloat16)
            out[:, at + HEAD : at + 2 * HEAD] = value.astype(jnp.bfloat16)


def project(inverse, feature, hidden, cosine, sine, gathered):
    _, tokens, depth = hidden.shape
    devices = inverse.shape[0]
    rows, width = depth // devices, gathered.shape[1]
    parts = min(devices, max(1, 1024 // rows))
    wide = parts * rows
    cols = width // devices

    def weight_spec(part):
        return pl.BlockSpec((rows, width), lambda i, inv, feat: (inv[i * parts + part], 0))

    table = pl.BlockSpec((tokens, HEAD), lambda i, inv, feat: (0, 0))
    out_width = 2 * HEAD * KV_HEADS // CHUNKS
    return pl.pallas_call(
        functools.partial(project_kernel, parts),
        out_shape=[jax.ShapeDtypeStruct((cols, depth), jnp.float32)]
        + [jax.ShapeDtypeStruct((tokens, out_width), jnp.bfloat16)] * CHUNKS,
        grid_spec=pltpu.PrefetchScalarGridSpec(
            num_scalar_prefetch=2,
            grid=(depth // wide,),
            in_specs=[pl.BlockSpec((None, tokens, wide), lambda i, inv, feat: (0, 0, i)), table, table]
            + [weight_spec(part) for part in range(parts)],
            out_specs=[pl.BlockSpec((cols, wide), lambda i, inv, feat: (0, i))]
            + [pl.BlockSpec((tokens, out_width), lambda i, inv, feat: (0, 0))] * CHUNKS,
            scratch_shapes=[pltpu.VMEM((tokens, width), jnp.float32)],
        ),
        compiler_params=pltpu.CompilerParams(vmem_limit_bytes=VMEM_LIMIT),
        cost_estimate=pl.CostEstimate(
            flops=2 * tokens * depth * width, bytes_accessed=2 * depth * (tokens + width), transcendentals=0
        ),
        name="project",
    )(inverse, feature, hidden, cosine, sine, *([gathered] * parts))


def attend_kernel(chunk, slots, own, q_ref, kv_ref, *refs):
    out_ref, keys, values = refs[-3:]
    half = q_ref.shape[0]
    seq = kv_ref.shape[0]
    wide = 2 * half
    segment = pl.program_id(1)

    @pl.when(segment == 0)
    def _():
        for place in range(seq // half):
            rows = pl.ds(pl.multiple_of(slots[place] * half, half), half)
            keys[place * half : (place + 1) * half] = kv_ref[rows, :HEAD]
            values[place * half : (place + 1) * half] = kv_ref[rows, HEAD:]

    index = own[segment]
    scale = math.log2(math.e) / math.sqrt(HEAD)

    def one_head(head, blocks, visible):
        at = pl.ds(pl.multiple_of(head * HEAD, HEAD), HEAD)
        query = q_ref[:, at]
        scores = []
        for block in range(blocks):
            score = lax.dot_general(
                query,
                keys[block * wide : (block + 1) * wide],
                (((1,), (1,)), ((), ())),
                preferred_element_type=jnp.float32,
            )
            scores.append(jnp.where(visible, score, -1e30) if block == blocks - 1 else score)
        best = jnp.max(functools.reduce(jnp.maximum, scores), axis=1, keepdims=True)
        weights = [jnp.exp2((score - best) * scale) for score in scores]
        summed = jnp.sum(functools.reduce(jnp.add, weights), axis=1, keepdims=True)
        result = functools.reduce(
            jnp.add,
            [
                jnp.dot(
                    weight.astype(jnp.bfloat16),
                    values[block * wide : (block + 1) * wide],
                    preferred_element_type=jnp.float32,
                )
                for block, weight in enumerate(weights)
            ],
        )
        out_ref[:, at] = (result / summed).astype(jnp.bfloat16)

    for blocks in range(1, seq // wide + 1):

        @pl.when(index // 2 + 1 == blocks)
        def _():
            row = lax.broadcasted_iota(jnp.int32, (half, wide), 0)
            visible = lax.broadcasted_iota(jnp.int32, (half, wide), 1) <= row + index % 2 * half

            def body(pair, carry):
                for head in range(2):
                    one_head(pair * 2 + head, blocks, visible)
                return carry

            lax.fori_loop(0, GROUPS // 2, body, 0)


def attend(chunk, slots, own, queries, gathered, earlier):
    _, tokens, width = queries.shape
    seq = gathered.shape[0]
    half = tokens // 2
    per = KV_HEADS // CHUNKS
    spec = pl.BlockSpec((None, half, GROUPS * HEAD), lambda g, s, slots, own: (0, s, chunk * per + g))
    more, specs, aliases = (), [], {}
    if earlier is not None:
        more, specs, aliases = (earlier,), [pl.BlockSpec(memory_space=pl.ANY)], {4: 0}
    return pl.pallas_call(
        functools.partial(attend_kernel, chunk),
        out_shape=jax.ShapeDtypeStruct(queries.shape, jnp.bfloat16),
        grid_spec=pltpu.PrefetchScalarGridSpec(
            num_scalar_prefetch=2,
            grid=(per, 2),
            in_specs=[spec, pl.BlockSpec((seq, 2 * HEAD), lambda g, s, slots, own: (0, g))] + specs,
            out_specs=spec,
            scratch_shapes=[pltpu.VMEM((seq, HEAD), jnp.bfloat16)] * 2,
        ),
        input_output_aliases=aliases,
        compiler_params=pltpu.CompilerParams(vmem_limit_bytes=VMEM_LIMIT),
        cost_estimate=pl.CostEstimate(
            flops=4 * tokens * seq * width // CHUNKS,
            bytes_accessed=4 * tokens * width // CHUNKS,
            transcendentals=tokens * seq * width // HEAD // CHUNKS // 2,
        ),
        name=f"attend{chunk}",
    )(slots, own, queries, gathered, *more)


def shards(
    hidden, queries, weights_old, gradient_old, first_old, second_old, old_owner, new_owner, offsets
):
    both = ("dp", "ctx")
    tokens = hidden.shape[1]
    half = tokens // 2
    first_next, second_next = moments(gradient_old, first_old, second_old)
    copies = update(weights_old, first_next, second_next).astype(jnp.bfloat16)
    gathered = lax.all_gather(copies, both, axis=0, tiled=True)
    outgoing = outgoing_moments(new_owner, gradient_old, first_old, second_old)
    incoming = lax.all_to_all(outgoing, both, split_axis=0, concat_axis=0, tiled=True)

    inverse = invert(old_owner)
    device = lax.axis_index(both)
    feature = lax.dynamic_slice(new_owner, (device,), (1,))
    starts = offsets[0] // half
    slots = invert(starts.reshape(-1))
    own = lax.dynamic_slice(starts, (lax.axis_index("ctx"), 0), (1, 2)).reshape(2)

    positions = (own[:, None] * half + jnp.arange(half, dtype=jnp.int32)[None, :]).reshape(tokens)
    exponent = jnp.arange(HEAD // 2, dtype=jnp.float32) * (2.0 / HEAD)
    inv_freq = jnp.power(rope_base, -exponent)
    angles = positions.astype(jnp.float32)[:, None] * inv_freq
    cosine, sine = jnp.cos(angles), jnp.sin(angles)
    cosine = jnp.concatenate([cosine, cosine], axis=1)
    sine = jnp.concatenate([-sine, sine], axis=1)

    weights_new, *chunks = project(inverse, feature, hidden, cosine, sine, gathered)
    whole = [lax.all_gather(chunk, "ctx", axis=0, tiled=True) for chunk in chunks]
    first_new, second_new = ordered_moments(inverse, incoming)
    attended = None
    for chunk in range(CHUNKS):
        attended = attend(chunk, slots, own, queries, whole[chunk], attended)
    return (weights_new, first_new, second_new, attended)


def solution(mesh):
    states = P(("dp", "ctx"), None)
    tokens = P("dp", "ctx", None)
    in_specs = (tokens, tokens, states, states, states, states, P(), P(), P("dp", None, None))
    out_specs = (states, states, states, tokens)
    return jax.shard_map(shards, mesh=mesh, in_specs=in_specs, out_specs=out_specs, check_vma=False)
```

```python
import functools
import math

import jax
import jax.numpy as jnp
from jax import lax
from jax.experimental import pallas as pl
from jax.experimental.pallas import tpu as pltpu
from jax.sharding import PartitionSpec as P

HEAD = 128
KV_HEADS = 4
Q_HEADS = 32
GROUPS = Q_HEADS // KV_HEADS
CHUNKS = 1
LANES = 128
VMEM_LIMIT = 48 * 1024 * 1024

learn_rate = 0.0003
beta_one = 0.9
beta_two = 0.95
adam_eps = 1e-08
decay_rate = 0.1
step_number = 1000
corr_one = 1.0 - beta_one**step_number
corr_two = 1.0 - beta_two**step_number
rope_base = 500000.0


def moments(gradient, first_mom, second_mom):
    first_next = beta_one * first_mom + (1.0 - beta_one) * gradient
    second_next = beta_two * second_mom + (1.0 - beta_two) * gradient * gradient
    return first_next, second_next


def update(weights, first_next, second_next):
    direction = first_next / corr_one / (jnp.sqrt(second_next / corr_two) + adam_eps)
    return weights - learn_rate * (direction + decay_rate * weights)


def invert(owners):
    ids = jnp.arange(owners.shape[0], dtype=jnp.int32)
    return jnp.sum(jnp.where(owners[None, :] == ids[:, None], ids[None, :], 0), axis=1)


def moments_kernel(new_owner, g_ref, m_ref, v_ref, out_ref, first_t, second_t):
    first_next, second_next = moments(g_ref[...], m_ref[...], v_ref[...])
    first_t[...] = first_next.T
    second_t[...] = second_next.T
    devices, both, _ = out_ref.shape
    cols = both // 2

    def body(dest, carry):
        rows = pl.ds(pl.multiple_of(new_owner[dest] * cols, cols), cols)
        out_ref[dest] = jnp.concatenate([first_t[rows], second_t[rows]], axis=0).astype(out_ref.dtype)
        return carry

    lax.fori_loop(0, devices, body, 0)


def outgoing_moments(new_owner, gradient, first_mom, second_mom):
    rows, width = gradient.shape
    devices = new_owner.shape[0]
    whole = pl.BlockSpec(memory_space=pltpu.VMEM)
    return pl.pallas_call(
        moments_kernel,
        out_shape=jax.ShapeDtypeStruct((devices, 2 * width // devices, rows), jnp.bfloat16),
        in_specs=[pl.BlockSpec(memory_space=pltpu.SMEM), whole, whole, whole],
        out_specs=whole,
        scratch_shapes=[pltpu.VMEM((width, rows), jnp.float32)] * 2,
        compiler_params=pltpu.CompilerParams(vmem_limit_bytes=VMEM_LIMIT),
        cost_estimate=pl.CostEstimate(flops=10 * rows * width, bytes_accessed=16 * rows * width, transcendentals=0),
        name="moments",
    )(new_owner, gradient, first_mom, second_mom)


def order_kernel(inverse, in_ref, first_ref, second_ref):
    devices, both, rows = in_ref.shape
    cols = both // 2
    for block in range(devices):
        value = in_ref[inverse[block]].astype(jnp.float32)
        first_ref[:, block * rows : (block + 1) * rows] = value[:cols]
        second_ref[:, block * rows : (block + 1) * rows] = value[cols:]


def ordered_moments(inverse, incoming):
    devices, both, rows = incoming.shape
    whole = pl.BlockSpec(memory_space=pltpu.VMEM)
    shape = jax.ShapeDtypeStruct((both // 2, devices * rows), jnp.float32)
    return pl.pallas_call(
        order_kernel,
        out_shape=(shape, shape),
        in_specs=[pl.BlockSpec(memory_space=pltpu.SMEM), whole],
        out_specs=(whole, whole),
        compiler_params=pltpu.CompilerParams(vmem_limit_bytes=VMEM_LIMIT),
        cost_estimate=pl.CostEstimate(flops=0, bytes_accessed=6 * devices * both * rows, transcendentals=0),
        name="order",
    )(inverse, incoming)


def project_kernel(parts, inverse, feature, hidden_ref, cos_ref, sin_ref, *refs):
    w_refs, new_ref, outs, total = refs[:parts], refs[parts], refs[parts + 1 : -1], refs[-1]
    step = pl.program_id(0)
    block = jnp.concatenate([w[...] for w in w_refs], axis=0)
    term = jnp.dot(hidden_ref[...], block, preferred_element_type=jnp.float32)

    @pl.when(step == 0)
    def _():
        total[...] = term

    @pl.when(step > 0)
    def _():
        total[...] += term

    cols = new_ref.shape[0]
    first = feature[0] * cols
    base = pl.multiple_of(first // LANES * LANES, LANES)
    lanes = jnp.concatenate([w[:, pl.ds(base, LANES)] for w in w_refs], axis=0)
    here = lax.broadcasted_iota(jnp.int32, (cols, LANES), 1)
    want = lax.broadcasted_iota(jnp.int32, (cols, LANES), 0) + (first - base)
    pick = (here == want).astype(jnp.float32).astype(jnp.bfloat16)
    new_ref[...] = lax.dot_general(pick, lanes, (((1,), (1,)), ((), ())), preferred_element_type=jnp.float32)

    @pl.when(step == pl.num_programs(0) - 1)
    def _():
        cosine, sine = cos_ref[...], sin_ref[...]
        per = KV_HEADS // len(outs)
        for head in range(KV_HEADS):
            key = total[:, head * HEAD : (head + 1) * HEAD]
            turned = jnp.concatenate([key[:, HEAD // 2 :], key[:, : HEAD // 2]], axis=1)
            value = total[:, (KV_HEADS + head) * HEAD : (KV_HEADS + head + 1) * HEAD]
            out, at = outs[head // per], head % per * 2 * HEAD
            out[:, at : at + HEAD] = (key * cosine + turned * sine).astype(jnp.bfloat16)
            out[:, at + HEAD : at + 2 * HEAD] = value.astype(jnp.bfloat16)


def project(inverse, feature, hidden, cosine, sine, gathered):
    _, tokens, depth = hidden.shape
    devices = inverse.shape[0]
    rows, width = depth // devices, gathered.shape[1]
    parts = min(devices, max(1, 2048 // rows))
    wide = parts * rows
    cols = width // devices

    def weight_spec(part):
        return pl.BlockSpec((rows, width), lambda i, inv, feat: (inv[i * parts + part], 0))

    table = pl.BlockSpec((tokens, HEAD), lambda i, inv, feat: (0, 0))
    out_width = 2 * HEAD * KV_HEADS // CHUNKS
    return pl.pallas_call(
        functools.partial(project_kernel, parts),
        out_shape=[jax.ShapeDtypeStruct((cols, depth), jnp.float32)]
        + [jax.ShapeDtypeStruct((tokens, out_width), jnp.bfloat16)] * CHUNKS,
        grid_spec=pltpu.PrefetchScalarGridSpec(
            num_scalar_prefetch=2,
            grid=(depth // wide,),
            in_specs=[pl.BlockSpec((None, tokens, wide), lambda i, inv, feat: (0, 0, i)), table, table]
            + [weight_spec(part) for part in range(parts)],
            out_specs=[pl.BlockSpec((cols, wide), lambda i, inv, feat: (0, i))]
            + [pl.BlockSpec((tokens, out_width), lambda i, inv, feat: (0, 0))] * CHUNKS,
            scratch_shapes=[pltpu.VMEM((tokens, width), jnp.float32)],
        ),
        compiler_params=pltpu.CompilerParams(vmem_limit_bytes=VMEM_LIMIT),
        cost_estimate=pl.CostEstimate(
            flops=2 * tokens * depth * width, bytes_accessed=2 * depth * (tokens + width), transcendentals=0
        ),
        name="project",
    )(inverse, feature, hidden, cosine, sine, *([gathered] * parts))


def attend_kernel(chunk, slots, own, q_ref, kv_ref, *refs):
    out_ref, keys, values = refs[-3:]
    half = q_ref.shape[0]
    seq = kv_ref.shape[0]
    wide = 2 * half
    segment = pl.program_id(1)

    @pl.when(segment == 0)
    def _():
        for place in range(seq // half):
            rows = pl.ds(pl.multiple_of(slots[place] * half, half), half)
            keys[place * half : (place + 1) * half] = kv_ref[rows, :HEAD]
            values[place * half : (place + 1) * half] = kv_ref[rows, HEAD:]

    index = own[segment]
    scale = math.log2(math.e) / math.sqrt(HEAD)

    def one_head(head, blocks, visible):
        at = pl.ds(pl.multiple_of(head * HEAD, HEAD), HEAD)
        query = q_ref[:, at]
        scores = []
        for block in range(blocks):
            score = lax.dot_general(
                query,
                keys[block * wide : (block + 1) * wide],
                (((1,), (1,)), ((), ())),
                preferred_element_type=jnp.float32,
            )
            scores.append(jnp.where(visible, score, -1e30) if block == blocks - 1 else score)
        best = jnp.max(functools.reduce(jnp.maximum, scores), axis=1, keepdims=True)
        weights = [jnp.exp2((score - best) * scale) for score in scores]
        summed = jnp.sum(functools.reduce(jnp.add, weights), axis=1, keepdims=True)
        result = functools.reduce(
            jnp.add,
            [
                jnp.dot(
                    weight.astype(jnp.bfloat16),
                    values[block * wide : (block + 1) * wide],
                    preferred_element_type=jnp.float32,
                )
                for block, weight in enumerate(weights)
            ],
        )
        out_ref[:, at] = (result / summed).astype(jnp.bfloat16)

    for blocks in range(1, seq // wide + 1):

        @pl.when(index // 2 + 1 == blocks)
        def _():
            row = lax.broadcasted_iota(jnp.int32, (half, wide), 0)
            visible = lax.broadcasted_iota(jnp.int32, (half, wide), 1) <= row + index % 2 * half

            def body(pair, carry):
                for head in range(4):
                    one_head(pair * 4 + head, blocks, visible)
                return carry

            lax.fori_loop(0, GROUPS // 4, body, 0)


def attend(chunk, slots, own, queries, gathered, earlier):
    _, tokens, width = queries.shape
    seq = gathered.shape[0]
    half = tokens // 2
    per = KV_HEADS // CHUNKS
    spec = pl.BlockSpec((None, half, GROUPS * HEAD), lambda g, s, slots, own: (0, s, chunk * per + g))
    more, specs, aliases = (), [], {}
    if earlier is not None:
        more, specs, aliases = (earlier,), [pl.BlockSpec(memory_space=pl.ANY)], {4: 0}
    return pl.pallas_call(
        functools.partial(attend_kernel, chunk),
        out_shape=jax.ShapeDtypeStruct(queries.shape, jnp.bfloat16),
        grid_spec=pltpu.PrefetchScalarGridSpec(
            num_scalar_prefetch=2,
            grid=(per, 2),
            in_specs=[spec, pl.BlockSpec((seq, 2 * HEAD), lambda g, s, slots, own: (0, g))] + specs,
            out_specs=spec,
            scratch_shapes=[pltpu.VMEM((seq, HEAD), jnp.bfloat16)] * 2,
        ),
        input_output_aliases=aliases,
        compiler_params=pltpu.CompilerParams(vmem_limit_bytes=VMEM_LIMIT),
        cost_estimate=pl.CostEstimate(
            flops=4 * tokens * seq * width // CHUNKS,
            bytes_accessed=4 * tokens * width // CHUNKS,
            transcendentals=tokens * seq * width // HEAD // CHUNKS // 2,
        ),
        name=f"attend{chunk}",
    )(slots, own, queries, gathered, *more)


def shards(
    hidden, queries, weights_old, gradient_old, first_old, second_old, old_owner, new_owner, offsets
):
    both = ("dp", "ctx")
    tokens = hidden.shape[1]
    half = tokens // 2
    first_next, second_next = moments(gradient_old, first_old, second_old)
    copies = update(weights_old, first_next, second_next).astype(jnp.bfloat16)
    gathered = lax.all_gather(copies, both, axis=0, tiled=True)
    outgoing = outgoing_moments(new_owner, gradient_old, first_old, second_old)
    incoming = lax.all_to_all(outgoing, both, split_axis=0, concat_axis=0, tiled=True)

    inverse = invert(old_owner)
    device = lax.axis_index(both)
    feature = lax.dynamic_slice(new_owner, (device,), (1,))
    starts = offsets[0] // half
    slots = invert(starts.reshape(-1))
    own = lax.dynamic_slice(starts, (lax.axis_index("ctx"), 0), (1, 2)).reshape(2)

    positions = (own[:, None] * half + jnp.arange(half, dtype=jnp.int32)[None, :]).reshape(tokens)
    exponent = jnp.arange(HEAD // 2, dtype=jnp.float32) * (2.0 / HEAD)
    inv_freq = jnp.power(rope_base, -exponent)
    angles = positions.astype(jnp.float32)[:, None] * inv_freq
    cosine, sine = jnp.cos(angles), jnp.sin(angles)
    cosine = jnp.concatenate([cosine, cosine], axis=1)
    sine = jnp.concatenate([-sine, sine], axis=1)

    hidden, incoming = lax.optimization_barrier((hidden, incoming))
    weights_new, *chunks = project(inverse, feature, hidden, cosine, sine, gathered)
    whole = [lax.all_gather(chunk, "ctx", axis=0, tiled=True) for chunk in chunks]
    first_new, second_new = ordered_moments(inverse, incoming)
    attended = None
    for chunk in range(CHUNKS):
        attended = attend(chunk, slots, own, queries, whole[chunk], attended)
    return (weights_new, first_new, second_new, attended)


def solution(mesh):
    states = P(("dp", "ctx"), None)
    tokens = P("dp", "ctx", None)
    in_specs = (tokens, tokens, states, states, states, states, P(), P(), P("dp", None, None))
    out_specs = (states, states, states, tokens)
    return jax.shard_map(shards, mesh=mesh, in_specs=in_specs, out_specs=out_specs, check_vma=False)
```
